128 devices in a mesh: blk: 16 (over x, y_hi, core), rep: 8 (over y_lo, z).
Axes of the slice: x: 4, y: 4 (y_hi: 2, y_lo: 2; y = y_hi * 2 + y_lo), z: 4, core: 2. Of those that a mesh axis runs over, the one named last changes fastest.
Arguments:
- user_factors: float32 [131072, 256], P(('blk', 'rep')), may hold values from -1.5 to 1.5
- user_first: float32 [131072, 256], P(('blk', 'rep')), may hold values from -6 to 6
- user_second: float32 [131072, 256], P(('blk', 'rep')), may hold values from 0.5 to 20
- item_factors: float32 [8192, 256], P(('blk', 'rep')), may hold values from -1.5 to 1.5
- item_first: float32 [8192, 256], P(('blk', 'rep')), may hold values from -6 to 6
- item_second: float32 [8192, 256], P(('blk', 'rep')), may hold values from 0.5 to 20
- block_rows: int32 [16, 8, 8, 8], P('blk', 'rep'), may hold values from 0 to 7, as said below
- block_cols: int32 [16, 8, 8, 8], P('blk', 'rep'), may hold values from 0 to 3
- live_slots: int32 [16, 8, 8], P('blk', 'rep'), may hold values from 2 to 8, as said below
- teacher: bfloat16 [16, 8, 8, 8, 128, 128], P('blk', 'rep'), may hold values from -6 to 6
Outputs:
- user_values: float32 [131072, 256], P(('blk', 'rep'))
- user_moment_one: float32 [131072, 256], P(('blk', 'rep'))
- user_moment_two: float32 [131072, 256], P(('blk', 'rep'))
- item_values: float32 [8192, 256], P(('blk', 'rep'))
- item_moment_one: float32 [8192, 256], P(('blk', 'rep'))
- item_moment_two: float32 [8192, 256], P(('blk', 'rep'))
The draws below stay inside these ranges and needn't reach their ends.
Inputs may be any that keep to these rules, and one draw needn't show every extreme that they name: For each (g, q, s) the 8 pairs (block_rows, block_cols) are distinct. `live_slots`: some entry equals 8 in every draw.
All inputs are finite; a program needn't handle non-finite values.
Results may differ from the reference program's by a relative error of at most 0.0034.
Values may be sent and summed in bfloat16 or wider, within the bound.
No kernel may reach another device: no remote copies, remote signals or barrier semaphores. Data moves between devices by JAX's collectives and lax.ppermute only.
A program may use at most 64 MiB of HBM per device.

```python
import math
import jax
import jax.numpy as jnp
from jax import lax

R = 256
BLK = 128
UB_DEV = 8
IB_GRP = 4
SLOTS = 8
STRATA = 8
USERS = 131072
ITEMS = 8192
N_BLK = 16
N_REP = 8


def pair_ids(key):
    count = N_BLK * N_REP * STRATA
    keys = jax.random.split(key, count)

    def one_list(single_key):
        return jax.random.permutation(single_key, UB_DEV * IB_GRP)[:SLOTS]
    chosen = jax.vmap(one_list)(keys)
    return chosen.reshape(N_BLK, N_REP, STRATA, SLOTS).astype(jnp.int32)


def draw_block_rows(key, part):
    return (pair_ids(key) // IB_GRP).astype(jnp.int32)


def draw_block_cols(key, part):
    return (pair_ids(key) % IB_GRP).astype(jnp.int32)


def draw_live_slots(key, part):
    key = jax.random.fold_in(key, 7)
    first_key, second_key = jax.random.split(key)
    total = N_BLK * N_REP * STRATA
    counts = jax.random.randint(first_key, (total,), SLOTS // 4, SLOTS + 1)
    where_full = jax.random.randint(second_key, (), 0, total)
    counts = counts.at[where_full].set(SLOTS)
    return counts.reshape(N_BLK, N_REP, STRATA).astype(jnp.int32)


def levels(key, shape, shards, low, top_value):
    factor_of, own = 1.0, jax.random.fold_in(key, 6)
    for axis_at, shards_of in shards:
        steps = jnp.exp(jax.random.uniform(jax.random.fold_in(own, axis_at), (shards_of,), jnp.float32, low / len(shards), top_value / len(shards)))
        factor_of = factor_of * jnp.repeat(steps, shape[axis_at] // shards_of).reshape([-1 if axis == axis_at else 1 for axis in range(len(shape))])
    return factor_of


def centred(key, shape, deviation, limit, shards=(), kind=jnp.bfloat16):
    factor_of = levels(key, shape, shards, -0.22, 0.18) if shards else 1.0
    array = jax.random.normal(key, shape, jnp.float32) * deviation * factor_of
    return jnp.minimum(jnp.maximum(array, -limit), limit).astype(kind)


def setup_inputs(seed: int = 0) -> dict:
    streams_of = jax.random.split(jax.random.key(seed), 11)
    return {
        "user_factors": centred(streams_of[0], (USERS, R), 0.25, 1.5, ((0, 128),), jnp.float32),
        "user_first": centred(streams_of[1], (USERS, R), 1.0, 6.0, ((0, 128),), jnp.float32),
        "user_second": jnp.clip(jnp.exp(math.log(20.0) - 3.6888795 * jax.random.uniform(streams_of[2], (USERS, R), jnp.float32) ** levels(streams_of[2], (USERS, R), ((0, 128),), -0.2, 0.2)), 0.5, 20.0),
        "item_factors": centred(streams_of[3], (ITEMS, R), 0.25, 1.5, ((0, 128),), jnp.float32),
        "item_first": centred(streams_of[4], (ITEMS, R), 1.0, 6.0, ((0, 128),), jnp.float32),
        "item_second": jnp.clip(jnp.exp(math.log(20.0) - 3.6888795 * jax.random.uniform(streams_of[5], (ITEMS, R), jnp.float32) ** levels(streams_of[5], (ITEMS, R), ((0, 128),), -0.2, 0.2)), 0.5, 20.0),
        "block_rows": draw_block_rows(jax.random.fold_in(streams_of[10], 71), 0),
        "block_cols": draw_block_cols(jax.random.fold_in(streams_of[10], 71), 0),
        "live_slots": draw_live_slots(jax.random.fold_in(streams_of[10], 71), 0),
        "teacher": centred(streams_of[9], (N_BLK, N_REP, STRATA, SLOTS, BLK, BLK), 1.0, 6.0, ((0, 16), (1, 8))),
    }


learn_rate = 0.01
adam_eps = 1e-08

def adam_update(values, moment_one, moment_two, gradient):
    moment_one = 0.9 * moment_one + 0.1 * gradient
    moment_two = 0.99 * moment_two + 0.01 * gradient * gradient
    values = values - learn_rate * moment_one / (jnp.sqrt(moment_two) + adam_eps)
    return (values, moment_one, moment_two)

def pick_blocks(table, index_list):
    return table[index_list]

def group_grads(packed):
    user_vals, item_vals, row_ids, col_ids, live_count, scores = packed
    user_bf = user_vals.astype(jnp.bfloat16)
    item_bf = item_vals.astype(jnp.bfloat16)
    user_blocks = jax.vmap(pick_blocks)(user_bf, row_ids).astype(jnp.float32)
    item_blocks = item_bf[col_ids].astype(jnp.float32)
    predicted = jnp.einsum('qsur,qsir->qsui', user_blocks, item_blocks)
    active = jnp.arange(SLOTS)[None, :] < live_count[:, None]
    residual = jnp.where(active[:, :, None, None], predicted - scores.astype(jnp.float32), 0.0).astype(jnp.bfloat16)
    residual = residual.astype(jnp.float32)
    user_terms = jnp.einsum('qsui,qsir->qsur', residual, item_blocks)
    item_terms = jnp.einsum('qsui,qsur->qsir', residual, user_blocks)

    def user_segments(terms, ids):
        return jax.ops.segment_sum(terms, ids, num_segments=UB_DEV)
    user_grad = jax.vmap(user_segments)(user_terms, row_ids)
    item_grad = jax.ops.segment_sum(item_terms.reshape(N_REP * SLOTS, BLK, R), col_ids.reshape(-1), num_segments=IB_GRP)
    return (user_grad, item_grad)

def reference(user_factors, user_first, user_second, item_factors, item_first, item_second, block_rows, block_cols, live_slots, teacher):
    user_shape = (N_BLK, N_REP, UB_DEV, BLK, R)
    item_shape = (N_BLK, IB_GRP, BLK, R)
    users = user_factors.reshape(user_shape)
    user_one = user_first.reshape(user_shape)
    user_two = user_second.reshape(user_shape)
    items = item_factors.reshape(item_shape)
    item_one = item_first.reshape(item_shape)
    item_two = item_second.reshape(item_shape)
    for stratum in range(STRATA):
        user_grad, item_grad = lax.map(group_grads, (users, items, block_rows[:, :, stratum], block_cols[:, :, stratum], live_slots[:, :, stratum], teacher[:, :, stratum]))
        users, user_one, user_two = adam_update(users, user_one, user_two, user_grad)
        items, item_one, item_two = adam_update(items, item_one, item_two, item_grad)
        items = jnp.roll(items, -1, axis=0)
        item_one = jnp.roll(item_one, -1, axis=0)
        item_two = jnp.roll(item_two, -1, axis=0)
    return (users.reshape(USERS, R), user_one.reshape(USERS, R), user_two.reshape(USERS, R), items.reshape(ITEMS, R), item_one.reshape(ITEMS, R), item_two.reshape(ITEMS, R))
```

```python
import functools

import jax
import jax.numpy as jnp
from jax import lax
from jax.experimental import pallas as pl
from jax.experimental.pallas import tpu as pltpu
from jax.sharding import PartitionSpec as P

learn_rate = 0.01
adam_eps = 1e-08
EDGE = 128
VMEM = pltpu.VMEM
F32 = jnp.float32
BF16 = jnp.bfloat16


def adam(values, moment_one, moment_two, gradient):
    moment_one = 0.9 * moment_one + 0.1 * gradient
    moment_two = 0.99 * moment_two + 0.01 * gradient * gradient
    values = values - learn_rate * moment_one / (jnp.sqrt(moment_two) + adam_eps)
    return values, moment_one, moment_two


def block_at(index):
    return pl.ds(pl.multiple_of(index * EDGE, EDGE), EDGE)


def item_grad_kernel(stratum, slots, meta, items, users, teacher, grad, residual):
    grad[...] = jnp.zeros_like(grad)
    live = meta[stratum, 2 * slots]
    for slot in range(slots):
        user_block = users[block_at(meta[stratum, slot]), :]
        col = block_at(meta[stratum, slots + slot])
        predicted = lax.dot_general(
            user_block, items[col, :], (((1,), (1,)), ((), ())), preferred_element_type=F32
        )
        left = jnp.where(slot < live, predicted - teacher[stratum, slot].astype(F32), 0.0).astype(BF16)
        residual[slot] = left
        grad[col, :] += lax.dot_general(
            left, user_block, (((0,), (0,)), ((), ())), preferred_element_type=F32
        )


def user_grads(stratum, slots, meta, items, residual, grad):
    grad[...] = jnp.zeros_like(grad)
    for slot in range(slots):
        col = block_at(meta[stratum, slots + slot])
        grad[meta[stratum, slot]] += jnp.dot(residual[slot], items[col, :], preferred_element_type=F32)


def user_kernel(stratum, slots, meta, items, residual, values, one, two, values_out, one_out, two_out, rounded, grad):
    user_grads(stratum, slots, meta, items, residual, grad)

    def one_block(at, carry):
        rows = block_at(at)
        new, first, second = adam(values[rows, :], one[rows, :], two[rows, :], grad[at])
        values_out[rows, :] = new
        one_out[rows, :] = first
        two_out[rows, :] = second
        rounded[rows, :] = new.astype(BF16)
        return carry

    lax.fori_loop(0, grad.shape[0], one_block, 0)


def last_user_kernel(stratum, slots, meta, items, residual, values, one, two, values_out, one_out, two_out, grad):
    at = pl.program_id(0)

    @pl.when(at == 0)
    def _():
        user_grads(stratum, slots, meta, items, residual, grad)

    values_out[...], one_out[...], two_out[...] = adam(values[...], one[...], two[...], grad[at])


def owner_kernel(parts, values, moments, values_out, moments_out):
    total = parts[0]
    for part in range(1, parts.shape[0]):
        total += parts[part]
    values_out[...], moments_out[0], moments_out[1] = adam(values[...], moments[0], moments[1], total)


def vmem_specs(count):
    return [pl.BlockSpec(memory_space=VMEM)] * count


def in_vmem(*arrays):
    return [pltpu.with_memory_space_constraint(a, VMEM) for a in arrays]


LIMIT = pltpu.CompilerParams(vmem_limit_bytes=6 * 1024 * 1024)

USER_COST = pl.CostEstimate(flops=300_000_000, bytes_accessed=8_000_000, transcendentals=600_000)


def on_device(
    user_factors,
    user_first,
    user_second,
    item_factors,
    item_first,
    item_second,
    block_rows,
    block_cols,
    live_slots,
    teacher,
):
    strata, slots = block_rows.shape[2], block_rows.shape[3]
    user_rows, rank = user_factors.shape
    shard = item_factors.shape[0]
    groups, reps = lax.axis_size("blk"), lax.axis_size("rep")
    half = reps // 2
    item_rows = shard * reps

    def owner(group, rep):
        return rep if group % 2 else (rep + half) % reps

    moves = [
        (group * reps + rep, ((group - 1) % groups) * reps + owner(group, rep))
        for group in range(groups)
        for rep in range(reps)
    ]

    def shifted(value):
        return lax.ppermute(value, ("blk", "rep"), moves)

    parity = lax.axis_index("blk") % 2
    turned = jnp.array(
        [[sum((p + hop) % 2 == 0 for hop in range(1, s + 1)) % 2 for s in range(strata)] for p in range(2)], jnp.int32
    )[parity]
    item_blocks = item_rows // EDGE
    cols = (block_cols[0, 0] + turned[:, None] * (item_blocks // 2)) % item_blocks
    meta = jnp.concatenate([block_rows[0, 0], cols, live_slots[0, 0][:, None]], axis=1)
    smem = pl.BlockSpec(memory_space=pltpu.SMEM)

    scores = teacher[0, 0]
    values, moments = item_factors, jnp.stack([item_first, item_second])
    users = (user_factors, user_first, user_second)
    user_bf = user_factors.astype(BF16)

    for stratum in range(strata):
        last = stratum == strata - 1
        copies = jnp.broadcast_to(values.astype(BF16)[None], (reps, shard, rank))
        items = lax.all_to_all(copies, "rep", 0, 0).reshape(item_rows, rank)
        grad, residual = pl.pallas_call(
            functools.partial(item_grad_kernel, stratum, slots),
            in_specs=[smem] + vmem_specs(3),
            out_specs=vmem_specs(2),
            out_shape=[VMEM((item_rows, rank), F32), VMEM((slots, EDGE, EDGE), BF16)],
            compiler_params=LIMIT,
            name="item_grad",
        )(meta, *in_vmem(items, user_bf, scores))
        parts = lax.all_to_all(grad.reshape(reps, shard, rank), "rep", 0, 0)
        values, moments = pl.pallas_call(
            owner_kernel,
            in_specs=vmem_specs(3),
            out_specs=vmem_specs(2),
            out_shape=[VMEM((shard, rank), F32), VMEM((2, shard, rank), F32)],
            compiler_params=LIMIT,
            name="owner_adam",
        )(*in_vmem(parts, values, moments))
        residual, values, moments = lax.optimization_barrier((residual, values, moments))
        values, moments = shifted(values), shifted(moments)
        operands = (meta, *in_vmem(items, residual))
        scratch = [VMEM((user_rows // EDGE, EDGE, rank), F32)]
        if last:
            by_block = pl.BlockSpec((EDGE, rank), lambda at: (at, 0))
            users = pl.pallas_call(
                functools.partial(last_user_kernel, stratum, slots),
                grid=(user_rows // EDGE,),
                in_specs=[smem] + vmem_specs(2) + [by_block] * 3,
                out_specs=[by_block] * 3,
                out_shape=[jax.ShapeDtypeStruct((user_rows, rank), F32)] * 3,
                scratch_shapes=scratch,
                compiler_params=LIMIT,
                cost_estimate=USER_COST,
                name="last_user_adam",
            )(*operands, *users)
        else:
            *users, user_bf = pl.pallas_call(
                functools.partial(user_kernel, stratum, slots),
                in_specs=[smem] + vmem_specs(5),
                out_specs=vmem_specs(4),
                out_shape=[VMEM((user_rows, rank), kind) for kind in (F32, F32, F32, BF16)],
                scratch_shapes=scratch,
                compiler_params=LIMIT,
                cost_estimate=USER_COST,
                name="user_adam",
            )(*operands, *in_vmem(*users))
            values, moments, user_bf = lax.optimization_barrier((values, moments, user_bf))

    return (*users, values, moments[0], moments[1])


def solution(mesh):
    rows = P(("blk", "rep"), None)
    in_specs = (rows,) * 6 + (
        P("blk", "rep", None, None),
        P("blk", "rep", None, None),
        P("blk", "rep", None),
        P("blk", "rep", None, None, None, None),
    )
    return jax.shard_map(on_device, mesh=mesh, in_specs=in_specs, out_specs=(rows,) * 6, check_vma=False)
```

```python
import functools

import jax
import jax.numpy as jnp
from jax import lax
from jax.experimental import pallas as pl
from jax.experimental.pallas import tpu as pltpu
from jax.sharding import PartitionSpec as P

learn_rate = 0.01
adam_eps = 1e-08
EDGE = 128
OWNERS = 4
VMEM = pltpu.VMEM
F32 = jnp.float32
BF16 = jnp.bfloat16


def adam(values, moment_one, moment_two, gradient):
    moment_one = 0.9 * moment_one + 0.1 * gradient
    moment_two = 0.99 * moment_two + 0.01 * gradient * gradient
    values = values - learn_rate * moment_one / (jnp.sqrt(moment_two) + adam_eps)
    return values, moment_one, moment_two


def block_at(index):
    return pl.ds(pl.multiple_of(index * EDGE, EDGE), EDGE)


def slot_grads(stratum, slots, meta, items, users, teacher, residual, grad):
    grad[...] = jnp.zeros_like(grad)
    live = meta[stratum, 2 * slots]
    for slot in range(slots):
        user_block = users[block_at(meta[stratum, slot]), :]
        col = block_at(meta[stratum, slots + slot])
        predicted = lax.dot_general(
            user_block, items[col, :], (((1,), (1,)), ((), ())), preferred_element_type=F32
        )
        left = jnp.where(slot < live, predicted - teacher[stratum, slot].astype(F32), 0.0).astype(BF16)
        residual[slot] = left
        grad[col, :] += lax.dot_general(
            left, user_block, (((0,), (0,)), ((), ())), preferred_element_type=F32
        )


def spread_parts(grad, parts):
    shard = parts.shape[1] // 2
    for owner in range(OWNERS):
        for side in range(2):
            at = (side * OWNERS + owner) * shard
            rows = grad[at : at + shard, :].astype(BF16)
            for copy in range(parts.shape[0] // OWNERS):
                parts[copy * OWNERS + owner, side * shard : (side + 1) * shard, :] = rows


def first_item_kernel(stratum, slots, meta, items, users, teacher, parts, residual, grad):
    slot_grads(stratum, slots, meta, items, users, teacher, residual, grad)
    spread_parts(grad, parts)


def item_kernel(stratum, slots, meta, *refs):
    got = refs[:OWNERS]
    users, teacher, parts, residual, items, grad = refs[OWNERS:]
    shard = got[0].shape[0] // 2
    place = meta[stratum, 2 * slots + 1]
    for hop in range(OWNERS):
        start = pl.multiple_of((place ^ hop) * shard, shard)
        items[pl.ds(start, shard), :] = got[hop][:shard, :]
        items[pl.ds(start + OWNERS * shard, shard), :] = got[hop][shard:, :]
    slot_grads(stratum, slots, meta, items, users, teacher, residual, grad)
    spread_parts(grad, parts)


def user_grads(stratum, slots, meta, items, residual, grad):
    grad[...] = jnp.zeros_like(grad)
    for slot in range(slots):
        col = block_at(meta[stratum, slots + slot])
        grad[meta[stratum, slot]] += jnp.dot(residual[slot], items[col, :], preferred_element_type=F32)


def user_kernel(stratum, slots, meta, items, residual, values, one, two, values_out, one_out, two_out, rounded, grad):
    user_grads(stratum, slots, meta, items, residual, grad)

    def one_block(at, carry):
        rows = block_at(at)
        new, first, second = adam(values[rows, :], one[rows, :], two[rows, :], grad[at])
        values_out[rows, :] = new
        one_out[rows, :] = first
        two_out[rows, :] = second
        rounded[rows, :] = new.astype(BF16)
        return carry

    lax.fori_loop(0, grad.shape[0], one_block, 0)


def last_user_kernel(stratum, slots, meta, items, residual, values, one, two, values_out, one_out, two_out, grad):
    at = pl.program_id(0)

    @pl.when(at == 0)
    def _():
        user_grads(stratum, slots, meta, items, residual, grad)

    values_out[...], one_out[...], two_out[...] = adam(
        values[...], one[...], two[...], grad[pl.ds(at * 2, 2)].reshape(values.shape)
    )


def owner_kernel(parts, state, state_out, rounded):
    total = parts[0].astype(F32)
    for part in range(1, parts.shape[0]):
        total += parts[part].astype(F32)
    new, state_out[1], state_out[2] = adam(state[0], state[1], state[2], total)
    state_out[0] = new
    rounded[...] = new.astype(BF16)


def first_owner_kernel(slots, meta, parts, own, other, state_out, rounded):
    total = parts[0].astype(F32)
    for part in range(1, parts.shape[0]):
        total += parts[part].astype(F32)

    def update(low, high):
        columns = [jnp.concatenate([low[term], high[term]], axis=0) for term in range(3)]
        new, state_out[1], state_out[2] = adam(*columns, total)
        state_out[0] = new
        rounded[...] = new.astype(BF16)

    side = meta[0, 2 * slots + 3]

    @pl.when(side == 0)
    def _():
        update(own, other)

    @pl.when(side == 1)
    def _():
        update(other, own)


def last_owner_kernel(stratum, slots, meta, parts, state, state_out):
    shard = state.shape[1] // 2
    rows = pl.ds(pl.multiple_of(meta[stratum, 2 * slots + 2] * shard, shard), shard)
    total = parts[0, rows, :].astype(F32)
    for part in range(1, parts.shape[0]):
        total += parts[part, rows, :].astype(F32)
    state_out[0], state_out[1], state_out[2] = adam(state[0, rows, :], state[1, rows, :], state[2, rows, :], total)


def start_kernel(values, one, two, own, arrived):
    moves = [
        pltpu.make_async_copy(source, own.at[term], arrived.at[term]) for term, source in enumerate((values, one, two))
    ]
    for move in moves:
        move.start()
    for move in moves:
        move.wait()


def finish_kernel(state, values, one, two, sent):
    moves = [
        pltpu.make_async_copy(state.at[term], target, sent.at[term]) for term, target in enumerate((values, one, two))
    ]
    for move in moves:
        move.start()
    for move in moves:
        move.wait()


def vmem_specs(count):
    return [pl.BlockSpec(memory_space=VMEM)] * count


def in_vmem(*arrays):
    return [pltpu.with_memory_space_constraint(a, VMEM) for a in arrays]


LIMIT = pltpu.CompilerParams(vmem_limit_bytes=6 * 1024 * 1024)
USER_COST = pl.CostEstimate(flops=300_000_000, bytes_accessed=8_000_000, transcendentals=600_000)


def on_device(
    user_factors,
    user_first,
    user_second,
    item_factors,
    item_first,
    item_second,
    block_rows,
    block_cols,
    live_slots,
    teacher,
):
    strata, slots = block_rows.shape[2], block_rows.shape[3]
    user_rows, rank = user_factors.shape
    shard = item_factors.shape[0]
    groups, reps = lax.axis_size("blk"), lax.axis_size("rep")
    item_rows = shard * reps

    def moves(hop):
        return [
            (group * reps + rep, ((group - 1) % groups) * reps + (rep ^ hop ^ (0 if group % 2 else OWNERS)))
            for group in range(groups)
            for rep in range(reps)
        ]

    def shifted(value, hop=0):
        return lax.ppermute(value, ("blk", "rep"), moves(hop))

    rep = lax.axis_index("rep")
    side = rep // OWNERS
    keep = (side + 1 - lax.axis_index("blk") % 2) % 2
    places = jnp.broadcast_to(jnp.stack([rep % OWNERS, keep, side]), (strata, 3))
    meta = jnp.concatenate([block_rows[0, 0], block_cols[0, 0], live_slots[0, 0][:, None], places], axis=1)
    smem = pl.BlockSpec(memory_space=pltpu.SMEM)

    scores = teacher[0, 0]
    users = (user_factors, user_first, user_second)
    user_bf = user_factors.astype(BF16)

    anywhere = pl.BlockSpec(memory_space=pl.ANY)
    own = pl.pallas_call(
        start_kernel,
        in_specs=[anywhere] * 3,
        out_specs=vmem_specs(1)[0],
        out_shape=VMEM((3, shard, rank), F32),
        scratch_shapes=[pltpu.SemaphoreType.DMA((3,))],
        compiler_params=LIMIT,
        name="start",
    )(*[pltpu.with_memory_space_constraint(a, pltpu.HBM) for a in (item_factors, item_first, item_second)])
    other = lax.ppermute(own, "rep", [(at, at ^ OWNERS) for at in range(reps)])
    copies = jnp.broadcast_to(own[0].astype(BF16)[None], (reps, shard, rank))
    items = lax.all_to_all(copies, "rep", 0, 0).reshape(item_rows, rank)
    items, own, other, user_bf, meta = lax.optimization_barrier((items, own, other, user_bf, meta))

    parts_shape = VMEM((reps, 2 * shard, rank), BF16)
    residual_shape = VMEM((slots, EDGE, EDGE), BF16)
    item_scratch = [VMEM((item_rows, rank), F32)]
    for stratum in range(strata):
        last = stratum == strata - 1
        if stratum == 0:
            parts, residual = pl.pallas_call(
                functools.partial(first_item_kernel, stratum, slots),
                in_specs=[smem] + vmem_specs(3),
                out_specs=vmem_specs(2),
                out_shape=[parts_shape, residual_shape],
                scratch_shapes=item_scratch,
                compiler_params=LIMIT,
                name="item_grad",
            )(meta, *in_vmem(items, user_bf, scores))
        else:
            parts, residual, items = pl.pallas_call(
                functools.partial(item_kernel, stratum, slots),
                in_specs=[smem] + vmem_specs(OWNERS + 2),
                out_specs=vmem_specs(3),
                out_shape=[parts_shape, residual_shape, VMEM((item_rows, rank), BF16)],
                scratch_shapes=item_scratch,
                compiler_params=LIMIT,
                name="item_grad",
            )(meta, *in_vmem(*got, user_bf, scores))
        if stratum > 0:
            parts, state = lax.optimization_barrier((parts, state))
        parts = lax.all_to_all(parts, "rep", 0, 0)
        scratch = [VMEM((user_rows // EDGE, EDGE, rank), F32)]
        if last:
            state = pl.pallas_call(
                functools.partial(last_owner_kernel, stratum, slots),
                in_specs=[smem] + vmem_specs(2),
                out_specs=vmem_specs(1)[0],
                out_shape=VMEM((3, shard, rank), F32),
                compiler_params=LIMIT,
                name="owner_adam",
            )(meta, *in_vmem(parts, state))
            residual, state = lax.optimization_barrier((residual, state))
            state = shifted(state)
            by_block = pl.BlockSpec((2 * EDGE, rank), lambda at: (at, 0))
            users = pl.pallas_call(
                functools.partial(last_user_kernel, stratum, slots),
                grid=(user_rows // (2 * EDGE),),
                in_specs=[smem] + vmem_specs(2) + [by_block] * 3,
                out_specs=[by_block] * 3,
                out_shape=[jax.ShapeDtypeStruct((user_rows, rank), F32)] * 3,
                scratch_shapes=scratch,
                compiler_params=LIMIT,
                cost_estimate=USER_COST,
                name="last_user_adam",
            )(meta, *in_vmem(items, residual), *users)
        else:
            first = stratum == 0
            state, rounded = pl.pallas_call(
                functools.partial(first_owner_kernel, slots) if first else owner_kernel,
                in_specs=[smem] * first + vmem_specs(3 if first else 2),
                out_specs=vmem_specs(2),
                out_shape=[VMEM((3, 2 * shard, rank), F32), VMEM((2 * shard, rank), BF16)],
                compiler_params=LIMIT,
                name="owner_adam",
            )(*[meta] * first, *in_vmem(parts, *((own, other) if first else (state,))))
            residual, rounded, state = lax.optimization_barrier((residual, rounded, state))
            state = shifted(state)
            got = [shifted(rounded, hop) for hop in reversed(range(OWNERS))][::-1]
            *users, user_bf = pl.pallas_call(
                functools.partial(user_kernel, stratum, slots),
                in_specs=[smem] + vmem_specs(5),
                out_specs=vmem_specs(4),
                out_shape=[VMEM((user_rows, rank), kind) for kind in (F32, F32, F32, BF16)],
                scratch_shapes=scratch,
                compiler_params=LIMIT,
                cost_estimate=USER_COST,
                name="user_adam",
            )(meta, *in_vmem(items, residual, *users))

    items = pl.pallas_call(
        finish_kernel,
        in_specs=vmem_specs(1),
        out_specs=[anywhere] * 3,
        out_shape=[pltpu.HBM((shard, rank), F32)] * 3,
        scratch_shapes=[pltpu.SemaphoreType.DMA((3,))],
        compiler_params=LIMIT,
        name="finish",
    )(*in_vmem(state))
    return (*users, *items)


def solution(mesh):
    rows = P(("blk", "rep"), None)
    in_specs = (rows,) * 6 + (
        P("blk", "rep", None, None),
        P("blk", "rep", None, None),
        P("blk", "rep", None),
        P("blk", "rep", None, None, None, None),
    )
    return jax.shard_map(on_device, mesh=mesh, in_specs=in_specs, out_specs=(rows,) * 6, check_vma=False)
```

```python
import functools

import jax
import jax.numpy as jnp
from jax import lax
from jax.experimental import pallas as pl
from jax.experimental.pallas import tpu as pltpu
from jax.sharding import PartitionSpec as P

learn_rate = 0.01
adam_eps = 1e-08
EDGE = 128
OWNERS = 4
VMEM = pltpu.VMEM
F32 = jnp.float32
BF16 = jnp.bfloat16


def adam(values, moment_one, moment_two, gradient):
    moment_one = 0.9 * moment_one + 0.1 * gradient
    moment_two = 0.99 * moment_two + 0.01 * gradient * gradient
    values = values - learn_rate * moment_one / (jnp.sqrt(moment_two) + adam_eps)
    return values, moment_one, moment_two


def words(meta, stratum):
    return meta[stratum, 0, 0], meta[stratum, 1, 0]


def field(word, at, bits):
    return (word >> at) & ((1 << bits) - 1)


def row_of(rows, slot):
    return field(rows, 3 * slot, 3)


def col_of(rest, slot):
    return block_at(field(rest, 2 * slot, 2))


def live_of(rest):
    return field(rest, 16, 4)


def place_of(rest):
    return field(rest, 20, 2)


def block_at(index):
    return pl.ds(pl.multiple_of(index * EDGE, EDGE), EDGE)


def slot_grads(stratum, slots, meta, items, users, teacher, residual, parts):
    shard = parts.shape[1] // 2
    rows, rest = words(meta, stratum)
    blocks = [users[block_at(row_of(rows, slot)), :] for slot in range(slots)]
    for slot, user_block in enumerate(blocks):
        predicted = lax.dot_general(
            items[col_of(rest, slot), :], user_block, (((1,), (1,)), ((), ())), preferred_element_type=F32
        )
        scores = teacher[stratum, slot].T.astype(F32)
        residual[slot] = jnp.where(slot < live_of(rest), predicted - scores, 0.0).astype(BF16)
    stacked = jnp.concatenate(blocks, axis=0)
    for block in range(items.shape[0] // EDGE):
        hits = [
            jnp.where(field(rest, 2 * slot, 2) == block, residual[slot], jnp.zeros((), BF16)) for slot in range(slots)
        ]
        grad = jnp.dot(jnp.concatenate(hits, axis=1), stacked, preferred_element_type=F32).astype(BF16)
        for piece in range(EDGE // shard):
            at = block * (EDGE // shard) + piece
            span = slice(at // OWNERS * shard, (at // OWNERS + 1) * shard)
            for owner in range(at % OWNERS, parts.shape[0], OWNERS):
                parts[owner, span, :] = grad[piece * shard : (piece + 1) * shard, :]


def first_item_kernel(stratum, slots, meta, items, users, teacher, parts, residual):
    slot_grads(stratum, slots, meta, items, users, teacher, residual, parts)


def item_kernel(stratum, slots, meta, *refs):
    got = refs[:OWNERS]
    users, teacher, parts, residual, items = refs[OWNERS:]
    shard = got[0].shape[0] // 2
    place = place_of(words(meta, stratum)[1])
    for hop in range(OWNERS):
        start = pl.multiple_of((place ^ hop) * shard, shard)
        items[pl.ds(start, shard), :] = got[hop][:shard, :]
        items[pl.ds(start + OWNERS * shard, shard), :] = got[hop][shard:, :]
    slot_grads(stratum, slots, meta, items, users, teacher, residual, parts)


def user_grads(stratum, slots, meta, items, residual, grad):
    grad[...] = jnp.zeros_like(grad)
    rows, rest = words(meta, stratum)
    for slot in range(slots):
        col = col_of(rest, slot)
        grad[row_of(rows, slot)] += lax.dot_general(
            residual[slot], items[col, :], (((0,), (0,)), ((), ())), preferred_element_type=F32
        )


def user_kernel(stratum, slots, meta, items, residual, values, one, two, values_out, one_out, two_out, rounded, grad):
    user_grads(stratum, slots, meta, items, residual, grad)

    def one_block(at, carry):
        rows = block_at(at)
        new, first, second = adam(values[rows, :], one[rows, :], two[rows, :], grad[at])
        values_out[rows, :] = new
        one_out[rows, :] = first
        two_out[rows, :] = second
        rounded[rows, :] = new.astype(BF16)
        return carry

    lax.fori_loop(0, grad.shape[0], one_block, 0)


def last_user_kernel(stratum, slots, meta, items, residual, values, one, two, values_out, one_out, two_out, grad):
    at = pl.program_id(0)

    @pl.when(at == 0)
    def _():
        user_grads(stratum, slots, meta, items, residual, grad)

    values_out[...], one_out[...], two_out[...] = adam(
        values[...], one[...], two[...], grad[pl.ds(at * 2, 2)].reshape(values.shape)
    )


def owner_kernel(parts, state, state_out, rounded):
    total = parts[0].astype(F32)
    for part in range(1, parts.shape[0]):
        total += parts[part].astype(F32)
    new, state_out[1], state_out[2] = adam(state[0], state[1], state[2], total)
    state_out[0] = new
    rounded[...] = new.astype(BF16)


def first_owner_kernel(slots, meta, parts, own, other, state_out, rounded):
    total = parts[0].astype(F32)
    for part in range(1, parts.shape[0]):
        total += parts[part].astype(F32)

    def update(low, high):
        columns = [jnp.concatenate([low[term], high[term]], axis=0) for term in range(3)]
        new, state_out[1], state_out[2] = adam(*columns, total)
        state_out[0] = new
        rounded[...] = new.astype(BF16)

    side = field(words(meta, 0)[1], 23, 1)

    @pl.when(side == 0)
    def _():
        update(own, other)

    @pl.when(side == 1)
    def _():
        update(other, own)


def last_owner_kernel(stratum, slots, meta, parts, state, state_out):
    shard = state.shape[1] // 2
    rows = pl.ds(pl.multiple_of(field(words(meta, stratum)[1], 22, 1) * shard, shard), shard)
    total = parts[0, rows, :].astype(F32)
    for part in range(1, parts.shape[0]):
        total += parts[part, rows, :].astype(F32)
    state_out[0], state_out[1], state_out[2] = adam(state[0, rows, :], state[1, rows, :], state[2, rows, :], total)


def start_kernel(values, one, two, own, arrived):
    moves = [
        pltpu.make_async_copy(source, own.at[term], arrived.at[term]) for term, source in enumerate((values, one, two))
    ]
    for move in moves:
        move.start()
    for move in moves:
        move.wait()


def finish_kernel(state, values, one, two, sent):
    moves = [
        pltpu.make_async_copy(state.at[term], target, sent.at[term]) for term, target in enumerate((values, one, two))
    ]
    for move in moves:
        move.start()
    for move in moves:
        move.wait()


def vmem_specs(count):
    return [pl.BlockSpec(memory_space=VMEM)] * count


def in_vmem(*arrays):
    return [pltpu.with_memory_space_constraint(a, VMEM) for a in arrays]


LIMIT = pltpu.CompilerParams(vmem_limit_bytes=6 * 1024 * 1024)
USER_COST = pl.CostEstimate(flops=300_000_000, bytes_accessed=8_000_000, transcendentals=600_000)


def on_device(
    user_factors,
    user_first,
    user_second,
    item_factors,
    item_first,
    item_second,
    block_rows,
    block_cols,
    live_slots,
    teacher,
):
    strata, slots = block_rows.shape[2], block_rows.shape[3]
    user_rows, rank = user_factors.shape
    shard = item_factors.shape[0]
    groups, reps = lax.axis_size("blk"), lax.axis_size("rep")
    item_rows = shard * reps

    def moves(hop):
        return [
            (group * reps + rep, ((group - 1) % groups) * reps + (rep ^ hop ^ (0 if group % 2 else OWNERS)))
            for group in range(groups)
            for rep in range(reps)
        ]

    def shifted(value, hop=0):
        return lax.ppermute(value, ("blk", "rep"), moves(hop))

    rep = lax.axis_index("rep")
    side = rep // OWNERS
    keep = (side + 1 - lax.axis_index("blk") % 2) % 2
    slot_at = jnp.arange(slots, dtype=jnp.int32)
    row_words = jnp.sum(block_rows[0, 0] << (3 * slot_at), axis=1)
    col_words = jnp.sum(block_cols[0, 0] << (2 * slot_at), axis=1)
    col_words += (live_slots[0, 0] << 16) + ((rep % OWNERS) << 20) + (keep << 22) + (side << 23)
    meta = jnp.broadcast_to(jnp.stack([row_words, col_words], axis=1)[:, :, None], (strata, 2, EDGE))

    scores = teacher[0, 0]
    users = (user_factors, user_first, user_second)
    user_bf = user_factors.astype(BF16)

    anywhere = pl.BlockSpec(memory_space=pl.ANY)
    own = pl.pallas_call(
        start_kernel,
        in_specs=[anywhere] * 3,
        out_specs=vmem_specs(1)[0],
        out_shape=VMEM((3, shard, rank), F32),
        scratch_shapes=[pltpu.SemaphoreType.DMA((3,))],
        compiler_params=LIMIT,
        name="start",
    )(*[pltpu.with_memory_space_constraint(a, pltpu.HBM) for a in (item_factors, item_first, item_second)])
    other = lax.ppermute(own, "rep", [(at, at ^ OWNERS) for at in range(reps)])
    copies = jnp.broadcast_to(own[0].astype(BF16)[None], (reps, shard, rank))
    items = lax.all_to_all(copies, "rep", 0, 0).reshape(item_rows, rank)
    items, own, other, user_bf, meta = lax.optimization_barrier((items, own, other, user_bf, meta))

    parts_shape = VMEM((reps, 2 * shard, rank), BF16)
    residual_shape = VMEM((slots, EDGE, EDGE), BF16)
    for stratum in range(strata):
        last = stratum == strata - 1
        if stratum == 0:
            parts, residual = pl.pallas_call(
                functools.partial(first_item_kernel, stratum, slots),
                in_specs=vmem_specs(1 + 3),
                out_specs=vmem_specs(2),
                out_shape=[parts_shape, residual_shape],
                compiler_params=LIMIT,
                name="item_grad",
            )(*in_vmem(meta, items, user_bf, scores))
        else:
            parts, residual, items = pl.pallas_call(
                functools.partial(item_kernel, stratum, slots),
                in_specs=vmem_specs(1 + OWNERS + 2),
                out_specs=vmem_specs(3),
                out_shape=[parts_shape, residual_shape, VMEM((item_rows, rank), BF16)],
                compiler_params=LIMIT,
                name="item_grad",
            )(*in_vmem(meta, *got, user_bf, scores))
        if stratum > 0:
            parts, state = lax.optimization_barrier((parts, state))
        parts = lax.all_to_all(parts, "rep", 0, 0)
        scratch = [VMEM((user_rows // EDGE, EDGE, rank), F32)]
        if last:
            state = pl.pallas_call(
                functools.partial(last_owner_kernel, stratum, slots),
                in_specs=vmem_specs(1 + 2),
                out_specs=vmem_specs(1)[0],
                out_shape=VMEM((3, shard, rank), F32),
                compiler_params=LIMIT,
                name="owner_adam",
            )(*in_vmem(meta, parts, state))
            residual, state = lax.optimization_barrier((residual, state))
            state = shifted(state)
            by_block = pl.BlockSpec((2 * EDGE, rank), lambda at: (at, 0))
            users = pl.pallas_call(
                functools.partial(last_user_kernel, stratum, slots),
                grid=(user_rows // (2 * EDGE),),
                in_specs=vmem_specs(1 + 2) + [by_block] * 3,
                out_specs=[by_block] * 3,
                out_shape=[jax.ShapeDtypeStruct((user_rows, rank), F32)] * 3,
                scratch_shapes=scratch,
                compiler_params=LIMIT,
                cost_estimate=USER_COST,
                name="last_user_adam",
            )(*in_vmem(meta, items, residual), *users)
        else:
            first = stratum == 0
            state, rounded = pl.pallas_call(
                functools.partial(first_owner_kernel, slots) if first else owner_kernel,
                in_specs=vmem_specs(4 if first else 2),
                out_specs=vmem_specs(2),
                out_shape=[VMEM((3, 2 * shard, rank), F32), VMEM((2 * shard, rank), BF16)],
                compiler_params=LIMIT,
                name="owner_adam",
            )(*in_vmem(*[meta] * first, parts, *((own, other) if first else (state,))))
            residual, rounded, state = lax.optimization_barrier((residual, rounded, state))
            state = shifted(state)
            got = [shifted(rounded, hop) for hop in reversed(range(OWNERS))][::-1]
            *users, user_bf = pl.pallas_call(
                functools.partial(user_kernel, stratum, slots),
                in_specs=vmem_specs(1 + 5),
                out_specs=vmem_specs(4),
                out_shape=[VMEM((user_rows, rank), kind) for kind in (F32, F32, F32, BF16)],
                scratch_shapes=scratch,
                compiler_params=LIMIT,
                cost_estimate=USER_COST,
                name="user_adam",
            )(*in_vmem(meta, items, residual, *users))

    items = pl.pallas_call(
        finish_kernel,
        in_specs=vmem_specs(1),
        out_specs=[anywhere] * 3,
        out_shape=[pltpu.HBM((shard, rank), F32)] * 3,
        scratch_shapes=[pltpu.SemaphoreType.DMA((3,))],
        compiler_params=LIMIT,
        name="finish",
    )(*in_vmem(state))
    return (*users, *items)


def solution(mesh):
    rows = P(("blk", "rep"), None)
    in_specs = (rows,) * 6 + (
        P("blk", "rep", None, None),
        P("blk", "rep", None, None),
        P("blk", "rep", None),
        P("blk", "rep", None, None, None, None),
    )
    return jax.shard_map(on_device, mesh=mesh, in_specs=in_specs, out_specs=(rows,) * 6, check_vma=False)
```

```python
import functools

import jax
import jax.numpy as jnp
from jax import lax
from jax.experimental import pallas as pl
from jax.experimental.pallas import tpu as pltpu
from jax.sharding import PartitionSpec as P

learn_rate = 0.01
adam_eps = 1e-08
EDGE = 128
OWNERS = 4
HOPS = (0, 2, 3, 1)
VMEM = pltpu.VMEM
F32 = jnp.float32
BF16 = jnp.bfloat16


def adam(values, moment_one, moment_two, gradient):
    moment_one = 0.9 * moment_one + 0.1 * gradient
    moment_two = 0.99 * moment_two + 0.01 * gradient * gradient
    values = values - learn_rate * moment_one / (jnp.sqrt(moment_two) + adam_eps)
    return values, moment_one, moment_two


def words(meta, stratum):
    return meta[stratum, 0, 0], meta[stratum, 1, 0]


def field(word, at, bits):
    return (word >> at) & ((1 << bits) - 1)


def row_of(rows, slot):
    return field(rows, 3 * slot, 3)


def col_of(rest, slot):
    return block_at(field(rest, 2 * slot, 2))


def live_of(rest):
    return field(rest, 16, 4)


def place_of(rest):
    return field(rest, 20, 2)


def block_at(index):
    return pl.ds(pl.multiple_of(index * EDGE, EDGE), EDGE)


def slot_grads(stratum, slots, meta, items, users, teacher, residual, parts):
    shard = parts.shape[1] // 2
    rows, rest = words(meta, stratum)
    blocks = [users[block_at(row_of(rows, slot)), :] for slot in range(slots)]
    for slot, user_block in enumerate(blocks):
        predicted = lax.dot_general(
            items[col_of(rest, slot), :], user_block, (((1,), (1,)), ((), ())), preferred_element_type=F32
        )
        scores = teacher[stratum, slot].T.astype(F32)
        residual[slot] = jnp.where(slot < live_of(rest), predicted - scores, 0.0).astype(BF16)
    stacked = jnp.concatenate(blocks, axis=0)
    for block in range(items.shape[0] // EDGE):
        hits = [
            jnp.where(field(rest, 2 * slot, 2) == block, residual[slot], jnp.zeros((), BF16)) for slot in range(slots)
        ]
        grad = jnp.dot(jnp.concatenate(hits, axis=1), stacked, preferred_element_type=F32).astype(BF16)
        for piece in range(EDGE // shard):
            at = block * (EDGE // shard) + piece
            span = slice(at // OWNERS * shard, (at // OWNERS + 1) * shard)
            for owner in range(at % OWNERS, parts.shape[0], OWNERS):
                parts[owner, span, :] = grad[piece * shard : (piece + 1) * shard, :]


def first_item_kernel(stratum, slots, meta, items, users, teacher, parts, residual):
    slot_grads(stratum, slots, meta, items, users, teacher, residual, parts)


def item_kernel(stratum, slots, meta, *refs):
    got = refs[:OWNERS]
    users, teacher, parts, residual, items = refs[OWNERS:]
    shard = items.shape[0] // (2 * OWNERS)
    place = place_of(words(meta, stratum)[1])
    for hop, piece in zip(HOPS, got):
        start = pl.multiple_of((place ^ hop) * shard, shard)
        for side in range(2):
            span = slice(side * shard, (side + 1) * shard)
            values = piece[span, :] if hop else piece[0, span, :].astype(BF16)
            items[pl.ds(start + side * OWNERS * shard, shard), :] = values
    slot_grads(stratum, slots, meta, items, users, teacher, residual, parts)


def user_grads(stratum, slots, meta, items, residual, grad):
    grad[...] = jnp.zeros_like(grad)
    rows, rest = words(meta, stratum)
    for slot in range(slots):
        col = col_of(rest, slot)
        grad[row_of(rows, slot)] += lax.dot_general(
            residual[slot], items[col, :], (((0,), (0,)), ((), ())), preferred_element_type=F32
        )


def user_kernel(stratum, slots, meta, items, residual, values, one, two, values_out, one_out, two_out, rounded, grad):
    user_grads(stratum, slots, meta, items, residual, grad)

    def one_block(at, carry):
        rows = block_at(at)
        new, first, second = adam(values[rows, :], one[rows, :], two[rows, :], grad[at])
        values_out[rows, :] = new
        one_out[rows, :] = first
        two_out[rows, :] = second
        rounded[rows, :] = new.astype(BF16)
        return carry

    lax.fori_loop(0, grad.shape[0], one_block, 0)


def last_user_kernel(stratum, slots, meta, items, residual, values, one, two, values_out, one_out, two_out, grad):
    at = pl.program_id(0)

    @pl.when(at == 0)
    def _():
        user_grads(stratum, slots, meta, items, residual, grad)

    values_out[...], one_out[...], two_out[...] = adam(
        values[...], one[...], two[...], grad[pl.ds(at * 2, 2)].reshape(values.shape)
    )


def owner_kernel(parts, state, state_out, rounded):
    total = parts[0].astype(F32)
    for part in range(1, parts.shape[0]):
        total += parts[part].astype(F32)
    new, state_out[1], state_out[2] = adam(state[0], state[1], state[2], total)
    state_out[0] = new
    rounded[...] = new.astype(BF16)


def first_owner_kernel(slots, meta, parts, own, other, state_out, rounded):
    total = parts[0].astype(F32)
    for part in range(1, parts.shape[0]):
        total += parts[part].astype(F32)

    def update(low, high):
        columns = [jnp.concatenate([low[term], high[term]], axis=0) for term in range(3)]
        new, state_out[1], state_out[2] = adam(*columns, total)
        state_out[0] = new
        rounded[...] = new.astype(BF16)

    side = field(words(meta, 0)[1], 23, 1)

    @pl.when(side == 0)
    def _():
        update(own, other)

    @pl.when(side == 1)
    def _():
        update(other, own)


def last_owner_kernel(stratum, slots, meta, parts, state, state_out):
    shard = state.shape[1] // 2
    rows = pl.ds(pl.multiple_of(field(words(meta, stratum)[1], 22, 1) * shard, shard), shard)
    total = parts[0, rows, :].astype(F32)
    for part in range(1, parts.shape[0]):
        total += parts[part, rows, :].astype(F32)
    state_out[0], state_out[1], state_out[2] = adam(state[0, rows, :], state[1, rows, :], state[2, rows, :], total)


def start_kernel(values, one, two, own, arrived):
    moves = [
        pltpu.make_async_copy(source, own.at[term], arrived.at[term]) for term, source in enumerate((values, one, two))
    ]
    for move in moves:
        move.start()
    for move in moves:
        move.wait()


def finish_kernel(state, values, one, two, sent):
    moves = [
        pltpu.make_async_copy(state.at[term], target, sent.at[term]) for term, target in enumerate((values, one, two))
    ]
    for move in moves:
        move.start()
    for move in moves:
        move.wait()


def vmem_specs(count):
    return [pl.BlockSpec(memory_space=VMEM)] * count


def in_vmem(*arrays):
    return [pltpu.with_memory_space_constraint(a, VMEM) for a in arrays]


LIMIT = pltpu.CompilerParams(vmem_limit_bytes=6 * 1024 * 1024)
USER_COST = pl.CostEstimate(flops=300_000_000, bytes_accessed=8_000_000, transcendentals=600_000)


def on_device(
    user_factors,
    user_first,
    user_second,
    item_factors,
    item_first,
    item_second,
    block_rows,
    block_cols,
    live_slots,
    teacher,
):
    strata, slots = block_rows.shape[2], block_rows.shape[3]
    user_rows, rank = user_factors.shape
    shard = item_factors.shape[0]
    groups, reps = lax.axis_size("blk"), lax.axis_size("rep")
    item_rows = shard * reps

    def moves(hop):
        return [
            (group * reps + rep, ((group - 1) % groups) * reps + (rep ^ hop ^ (0 if group % 2 else OWNERS)))
            for group in range(groups)
            for rep in range(reps)
        ]

    def shifted(value, hop=0):
        return lax.ppermute(value, ("blk", "rep"), moves(hop))

    rep = lax.axis_index("rep")
    side = rep // OWNERS
    keep = (side + 1 - lax.axis_index("blk") % 2) % 2
    slot_at = jnp.arange(slots, dtype=jnp.int32)
    row_words = jnp.sum(block_rows[0, 0] << (3 * slot_at), axis=1)
    col_words = jnp.sum(block_cols[0, 0] << (2 * slot_at), axis=1)
    col_words += (live_slots[0, 0] << 16) + ((rep % OWNERS) << 20) + (keep << 22) + (side << 23)
    meta = jnp.broadcast_to(jnp.stack([row_words, col_words], axis=1)[:, :, None], (strata, 2, EDGE))

    scores = teacher[0, 0]
    users = (user_factors, user_first, user_second)
    user_bf = user_factors.astype(BF16)

    anywhere = pl.BlockSpec(memory_space=pl.ANY)
    own = pl.pallas_call(
        start_kernel,
        in_specs=[anywhere] * 3,
        out_specs=vmem_specs(1)[0],
        out_shape=VMEM((3, shard, rank), F32),
        scratch_shapes=[pltpu.SemaphoreType.DMA((3,))],
        compiler_params=LIMIT,
        name="start",
    )(*[pltpu.with_memory_space_constraint(a, pltpu.HBM) for a in (item_factors, item_first, item_second)])
    other = lax.ppermute(own, "rep", [(at, at ^ OWNERS) for at in range(reps)])
    copies = jnp.broadcast_to(own[0].astype(BF16)[None], (reps, shard, rank))
    items = lax.all_to_all(copies, "rep", 0, 0).reshape(item_rows, rank)
    items, own, other, user_bf, meta = lax.optimization_barrier((items, own, other, user_bf, meta))

    parts_shape = VMEM((reps, 2 * shard, rank), BF16)
    residual_shape = VMEM((slots, EDGE, EDGE), BF16)
    for stratum in range(strata):
        last = stratum == strata - 1
        if stratum == 0:
            parts, residual = pl.pallas_call(
                functools.partial(first_item_kernel, stratum, slots),
                in_specs=vmem_specs(1 + 3),
                out_specs=vmem_specs(2),
                out_shape=[parts_shape, residual_shape],
                compiler_params=LIMIT,
                name="item_grad",
            )(*in_vmem(meta, items, user_bf, scores))
        else:
            parts, residual, items = pl.pallas_call(
                functools.partial(item_kernel, stratum, slots),
                in_specs=vmem_specs(1 + OWNERS + 2),
                out_specs=vmem_specs(3),
                out_shape=[parts_shape, residual_shape, VMEM((item_rows, rank), BF16)],
                compiler_params=LIMIT,
                name="item_grad",
            )(*in_vmem(meta, *got, user_bf, scores))
        parts = lax.all_to_all(parts, "rep", 0, 0)
        scratch = [VMEM((user_rows // EDGE, EDGE, rank), F32)]
        if last:
            state = pl.pallas_call(
                functools.partial(last_owner_kernel, stratum, slots),
                in_specs=vmem_specs(1 + 2),
                out_specs=vmem_specs(1)[0],
                out_shape=VMEM((3, shard, rank), F32),
                compiler_params=LIMIT,
                name="owner_adam",
            )(*in_vmem(meta, parts, state))
            residual, state = lax.optimization_barrier((residual, state))
            state = shifted(state)
            by_block = pl.BlockSpec((2 * EDGE, rank), lambda at: (at, 0))
            users = pl.pallas_call(
                functools.partial(last_user_kernel, stratum, slots),
                grid=(user_rows // (2 * EDGE),),
                in_specs=vmem_specs(1 + 2) + [by_block] * 3,
                out_specs=[by_block] * 3,
                out_shape=[jax.ShapeDtypeStruct((user_rows, rank), F32)] * 3,
                scratch_shapes=scratch,
                compiler_params=LIMIT,
                cost_estimate=USER_COST,
                name="last_user_adam",
            )(*in_vmem(meta, items, residual), *users)
        else:
            first = stratum == 0
            state, rounded = pl.pallas_call(
                functools.partial(first_owner_kernel, slots) if first else owner_kernel,
                in_specs=vmem_specs(4 if first else 2),
                out_specs=vmem_specs(2),
                out_shape=[VMEM((3, 2 * shard, rank), F32), VMEM((2 * shard, rank), BF16)],
                compiler_params=LIMIT,
                name="owner_adam",
            )(*in_vmem(*[meta] * first, parts, *((own, other) if first else (state,))))
            residual, rounded, state = lax.optimization_barrier((residual, rounded, state))
            got = [shifted(rounded, hop) if hop else None for hop in HOPS]
            state = shifted(state)
            got[HOPS.index(0)] = state
            *users, user_bf = pl.pallas_call(
                functools.partial(user_kernel, stratum, slots),
                in_specs=vmem_specs(1 + 5),
                out_specs=vmem_specs(4),
                out_shape=[VMEM((user_rows, rank), kind) for kind in (F32, F32, F32, BF16)],
                scratch_shapes=scratch,
                compiler_params=LIMIT,
                cost_estimate=USER_COST,
                name="user_adam",
            )(*in_vmem(meta, items, residual, *users))

    items = pl.pallas_call(
        finish_kernel,
        in_specs=vmem_specs(1),
        out_specs=[anywhere] * 3,
        out_shape=[pltpu.HBM((shard, rank), F32)] * 3,
        scratch_shapes=[pltpu.SemaphoreType.DMA((3,))],
        compiler_params=LIMIT,
        name="finish",
    )(*in_vmem(state))
    return (*users, *items)


def solution(mesh):
    rows = P(("blk", "rep"), None)
    in_specs = (rows,) * 6 + (
        P("blk", "rep", None, None),
        P("blk", "rep", None, None),
        P("blk", "rep", None),
        P("blk", "rep", None, None, None, None),
    )
    return jax.shard_map(on_device, mesh=mesh, in_specs=in_specs, out_specs=(rows,) * 6, check_vma=False)
```

```python
import functools

import jax
import jax.numpy as jnp
from jax import lax
from jax.experimental import pallas as pl
from jax.experimental.pallas import tpu as pltpu
from jax.sharding import PartitionSpec as P

learn_rate = 0.01
adam_eps = 1e-08
EDGE = 128
OWNERS = 4
SUM_HOPS = (2, 3, 1)
HOPS = (0, 2, 3, 1)
VMEM = pltpu.VMEM
F32 = jnp.float32
BF16 = jnp.bfloat16


def adam(values, moment_one, moment_two, gradient):
    moment_one = 0.9 * moment_one + 0.1 * gradient
    moment_two = 0.99 * moment_two + 0.01 * gradient * gradient
    values = values - learn_rate * moment_one / (jnp.sqrt(moment_two) + adam_eps)
    return values, moment_one, moment_two


def words(meta, stratum):
    return meta[stratum, 0, 0], meta[stratum, 1, 0]


def field(word, at, bits):
    return (word >> at) & ((1 << bits) - 1)


def row_of(rows, slot):
    return field(rows, 3 * slot, 3)


def col_of(rest, slot):
    return block_at(field(rest, 2 * slot, 2))


def live_of(rest):
    return field(rest, 16, 4)


def place_of(rest):
    return field(rest, 20, 2)


def block_at(index):
    return pl.ds(pl.multiple_of(index * EDGE, EDGE), EDGE)


def slot_grads(stratum, slots, meta, items, users, teacher, residual, grad):
    rows, rest = words(meta, stratum)
    blocks = [users[block_at(row_of(rows, slot)), :] for slot in range(slots)]
    for slot, user_block in enumerate(blocks):
        predicted = lax.dot_general(
            items[col_of(rest, slot), :], user_block, (((1,), (1,)), ((), ())), preferred_element_type=F32
        )
        scores = teacher[stratum, slot].T.astype(F32)
        residual[slot] = jnp.where(slot < live_of(rest), predicted - scores, 0.0).astype(BF16)
    stacked = jnp.concatenate(blocks, axis=0)
    for block in range(items.shape[0] // EDGE):
        hits = [
            jnp.where(field(rest, 2 * slot, 2) == block, residual[slot], jnp.zeros((), BF16)) for slot in range(slots)
        ]
        grad[block * EDGE : (block + 1) * EDGE, :] = jnp.dot(
            jnp.concatenate(hits, axis=1), stacked, preferred_element_type=F32
        )


def split_parts(place, grad, mine, *sent):
    shard = mine.shape[0] // 2
    for hop, part in zip((0, *SUM_HOPS), (mine, *sent)):
        start = pl.multiple_of((place ^ hop) * shard, shard)
        for side in range(2):
            rows = grad[pl.ds(start + side * OWNERS * shard, shard), :]
            part[side * shard : (side + 1) * shard, :] = rows.astype(part.dtype)


def first_item_kernel(stratum, slots, meta, items, users, teacher, *refs):
    *parts, residual, grad = refs
    slot_grads(stratum, slots, meta, items, users, teacher, residual, grad)
    split_parts(place_of(words(meta, stratum)[1]), grad, *parts)


def item_kernel(stratum, slots, meta, *refs):
    got = refs[:OWNERS]
    users, teacher, *parts, residual, items, grad = refs[OWNERS:]
    shard = items.shape[0] // (2 * OWNERS)
    place = place_of(words(meta, stratum)[1])
    for hop, piece in zip(HOPS, got):
        start = pl.multiple_of((place ^ hop) * shard, shard)
        for side in range(2):
            span = slice(side * shard, (side + 1) * shard)
            values = piece[span, :] if hop else piece[0, span, :].astype(BF16)
            items[pl.ds(start + side * OWNERS * shard, shard), :] = values
    slot_grads(stratum, slots, meta, items, users, teacher, residual, grad)
    split_parts(place, grad, *parts)


def user_grads(stratum, slots, meta, items, residual, grad):
    grad[...] = jnp.zeros_like(grad)
    rows, rest = words(meta, stratum)
    for slot in range(slots):
        col = col_of(rest, slot)
        grad[row_of(rows, slot)] += lax.dot_general(
            residual[slot], items[col, :], (((0,), (0,)), ((), ())), preferred_element_type=F32
        )


def user_kernel(stratum, slots, meta, items, residual, values, one, two, values_out, one_out, two_out, rounded, grad):
    user_grads(stratum, slots, meta, items, residual, grad)

    def one_block(at, carry):
        rows = block_at(at)
        new, first, second = adam(values[rows, :], one[rows, :], two[rows, :], grad[at])
        values_out[rows, :] = new
        one_out[rows, :] = first
        two_out[rows, :] = second
        rounded[rows, :] = new.astype(BF16)
        return carry

    lax.fori_loop(0, grad.shape[0], one_block, 0)


def last_user_kernel(stratum, slots, meta, items, residual, values, one, two, values_out, one_out, two_out, grad):
    at = pl.program_id(0)

    @pl.when(at == 0)
    def _():
        user_grads(stratum, slots, meta, items, residual, grad)

    values_out[...], one_out[...], two_out[...] = adam(
        values[...], one[...], two[...], grad[pl.ds(at * 2, 2)].reshape(values.shape)
    )


def sum_kernel(*refs):
    *parts, total = refs
    acc = parts[0][...]
    for part in parts[1:]:
        acc += part[...].astype(F32)
    total[...] = acc.astype(total.dtype)


def owner_kernel(mine, other, state, state_out, rounded):
    total = mine[...].astype(F32) + other[...].astype(F32)
    new, state_out[1], state_out[2] = adam(state[0], state[1], state[2], total)
    state_out[0] = new
    rounded[...] = new.astype(BF16)


def last_owner_kernel(stratum, slots, meta, mine, other, state, state_out):
    shard = state.shape[1] // 2
    rows = pl.ds(pl.multiple_of(field(words(meta, stratum)[1], 22, 1) * shard, shard), shard)
    total = mine[rows, :].astype(F32) + other[rows, :].astype(F32)
    state_out[0], state_out[1], state_out[2] = adam(state[0, rows, :], state[1, rows, :], state[2, rows, :], total)


def first_owner_kernel(slots, meta, mine, other_part, own, other, state_out, rounded):
    total = mine[...].astype(F32) + other_part[...].astype(F32)

    def update(low, high):
        columns = [jnp.concatenate([low[term], high[term]], axis=0) for term in range(3)]
        new, state_out[1], state_out[2] = adam(*columns, total)
        state_out[0] = new
        rounded[...] = new.astype(BF16)

    side = field(words(meta, 0)[1], 23, 1)

    @pl.when(side == 0)
    def _():
        update(own, other)

    @pl.when(side == 1)
    def _():
        update(other, own)


def start_kernel(values, one, two, own, arrived):
    moves = [
        pltpu.make_async_copy(source, own.at[term], arrived.at[term]) for term, source in enumerate((values, one, two))
    ]
    for move in moves:
        move.start()
    for move in moves:
        move.wait()


def finish_kernel(state, values, one, two, sent):
    moves = [
        pltpu.make_async_copy(state.at[term], target, sent.at[term]) for term, target in enumerate((values, one, two))
    ]
    for move in moves:
        move.start()
    for move in moves:
        move.wait()


def vmem_specs(count):
    return [pl.BlockSpec(memory_space=VMEM)] * count


def in_vmem(*arrays):
    return [pltpu.with_memory_space_constraint(a, VMEM) for a in arrays]


LIMIT = pltpu.CompilerParams(vmem_limit_bytes=6 * 1024 * 1024)
USER_COST = pl.CostEstimate(flops=300_000_000, bytes_accessed=8_000_000, transcendentals=600_000)


def on_device(
    user_factors,
    user_first,
    user_second,
    item_factors,
    item_first,
    item_second,
    block_rows,
    block_cols,
    live_slots,
    teacher,
):
    strata, slots = block_rows.shape[2], block_rows.shape[3]
    user_rows, rank = user_factors.shape
    shard = item_factors.shape[0]
    groups, reps = lax.axis_size("blk"), lax.axis_size("rep")
    item_rows = shard * reps

    def moves(hop):
        return [
            (group * reps + rep, ((group - 1) % groups) * reps + (rep ^ hop ^ (0 if group % 2 else OWNERS)))
            for group in range(groups)
            for rep in range(reps)
        ]

    def shifted(value, hop=0):
        return lax.ppermute(value, ("blk", "rep"), moves(hop))

    rep = lax.axis_index("rep")
    side = rep // OWNERS
    keep = (side + 1 - lax.axis_index("blk") % 2) % 2
    slot_at = jnp.arange(slots, dtype=jnp.int32)
    row_words = jnp.sum(block_rows[0, 0] << (3 * slot_at), axis=1)
    col_words = jnp.sum(block_cols[0, 0] << (2 * slot_at), axis=1)
    col_words += (live_slots[0, 0] << 16) + ((rep % OWNERS) << 20) + (keep << 22) + (side << 23)
    meta = jnp.broadcast_to(jnp.stack([row_words, col_words], axis=1)[:, :, None], (strata, 2, EDGE))

    scores = teacher[0, 0]
    users = (user_factors, user_first, user_second)
    user_bf = user_factors.astype(BF16)

    anywhere = pl.BlockSpec(memory_space=pl.ANY)
    own = pl.pallas_call(
        start_kernel,
        in_specs=[anywhere] * 3,
        out_specs=vmem_specs(1)[0],
        out_shape=VMEM((3, shard, rank), F32),
        scratch_shapes=[pltpu.SemaphoreType.DMA((3,))],
        compiler_params=LIMIT,
        name="start",
    )(*[pltpu.with_memory_space_constraint(a, pltpu.HBM) for a in (item_factors, item_first, item_second)])
    other = lax.ppermute(own, "rep", [(at, at ^ OWNERS) for at in range(reps)])
    copies = jnp.broadcast_to(own[0].astype(BF16)[None], (reps, shard, rank))
    items = lax.all_to_all(copies, "rep", 0, 0).reshape(item_rows, rank)
    items, own, other, user_bf, meta = lax.optimization_barrier((items, own, other, user_bf, meta))

    parts_shape = [VMEM((2 * shard, rank), F32)] + [VMEM((2 * shard, rank), BF16)] * (OWNERS - 1)
    item_scratch = [VMEM((item_rows, rank), F32)]
    residual_shape = VMEM((slots, EDGE, EDGE), BF16)
    for stratum in range(strata):
        last = stratum == strata - 1
        if stratum == 0:
            *parts, residual = pl.pallas_call(
                functools.partial(first_item_kernel, stratum, slots),
                in_specs=vmem_specs(1 + 3),
                out_specs=vmem_specs(OWNERS + 1),
                out_shape=[*parts_shape, residual_shape],
                scratch_shapes=item_scratch,
                compiler_params=LIMIT,
                name="item_grad",
            )(*in_vmem(meta, items, user_bf, scores))
        else:
            *parts, residual, items = pl.pallas_call(
                functools.partial(item_kernel, stratum, slots),
                in_specs=vmem_specs(1 + OWNERS + 2),
                out_specs=vmem_specs(OWNERS + 2),
                out_shape=[*parts_shape, residual_shape, VMEM((item_rows, rank), BF16)],
                scratch_shapes=item_scratch,
                compiler_params=LIMIT,
                name="item_grad",
            )(*in_vmem(meta, *got, user_bf, scores))
        for at, hop in enumerate(SUM_HOPS):
            parts[at + 1] = lax.ppermute(parts[at + 1], "rep", [(rep, rep ^ hop) for rep in range(reps)])
        mine = pl.pallas_call(
            sum_kernel,
            in_specs=vmem_specs(OWNERS),
            out_specs=vmem_specs(1)[0],
            out_shape=VMEM((2 * shard, rank), BF16),
            compiler_params=LIMIT,
            name="sum_parts",
        )(*in_vmem(*parts))
        partner = lax.ppermute(mine, "rep", [(at, at ^ OWNERS) for at in range(reps)])
        scratch = [VMEM((user_rows // EDGE, EDGE, rank), F32)]
        if last:
            state = pl.pallas_call(
                functools.partial(last_owner_kernel, stratum, slots),
                in_specs=vmem_specs(1 + 3),
                out_specs=vmem_specs(1)[0],
                out_shape=VMEM((3, shard, rank), F32),
                compiler_params=LIMIT,
                name="owner_adam",
            )(*in_vmem(meta, mine, partner, state))
            residual, state = lax.optimization_barrier((residual, state))
            state = shifted(state)
            by_block = pl.BlockSpec((2 * EDGE, rank), lambda at: (at, 0))
            users = pl.pallas_call(
                functools.partial(last_user_kernel, stratum, slots),
                grid=(user_rows // (2 * EDGE),),
                in_specs=vmem_specs(1 + 2) + [by_block] * 3,
                out_specs=[by_block] * 3,
                out_shape=[jax.ShapeDtypeStruct((user_rows, rank), F32)] * 3,
                scratch_shapes=scratch,
                compiler_params=LIMIT,
                cost_estimate=USER_COST,
                name="last_user_adam",
            )(*in_vmem(meta, items, residual), *users)
        else:
            first = stratum == 0
            state, rounded = pl.pallas_call(
                functools.partial(first_owner_kernel, slots) if first else owner_kernel,
                in_specs=vmem_specs(5 if first else 3),
                out_specs=vmem_specs(2),
                out_shape=[VMEM((3, 2 * shard, rank), F32), VMEM((2 * shard, rank), BF16)],
                compiler_params=LIMIT,
                name="owner_adam",
            )(*in_vmem(*[meta] * first, mine, partner, *((own, other) if first else (state,))))
            residual, rounded, state = lax.optimization_barrier((residual, rounded, state))
            got = [shifted(rounded, hop) if hop else None for hop in HOPS]
            state = shifted(state)
            got[HOPS.index(0)] = state
            *users, user_bf = pl.pallas_call(
                functools.partial(user_kernel, stratum, slots),
                in_specs=vmem_specs(1 + 5),
                out_specs=vmem_specs(4),
                out_shape=[VMEM((user_rows, rank), kind) for kind in (F32, F32, F32, BF16)],
                scratch_shapes=scratch,
                compiler_params=LIMIT,
                cost_estimate=USER_COST,
                name="user_adam",
            )(*in_vmem(meta, items, residual, *users))

    items = pl.pallas_call(
        finish_kernel,
        in_specs=vmem_specs(1),
        out_specs=[anywhere] * 3,
        out_shape=[pltpu.HBM((shard, rank), F32)] * 3,
        scratch_shapes=[pltpu.SemaphoreType.DMA((3,))],
        compiler_params=LIMIT,
        name="finish",
    )(*in_vmem(state))
    return (*users, *items)


def solution(mesh):
    rows = P(("blk", "rep"), None)
    in_specs = (rows,) * 6 + (
        P("blk", "rep", None, None),
        P("blk", "rep", None, None),
        P("blk", "rep", None),
        P("blk", "rep", None, None, None, None),
    )
    return jax.shard_map(on_device, mesh=mesh, in_specs=in_specs, out_specs=(rows,) * 6, check_vma=False)
```

```python
import functools

import jax
import jax.numpy as jnp
from jax import lax
from jax.experimental import pallas as pl
from jax.experimental.pallas import tpu as pltpu
from jax.sharding import PartitionSpec as P

learn_rate = 0.01
adam_eps = 1e-08
EDGE = 128
OWNERS = 4
SUM_HOPS = (2, 3, 1)
HOPS = (0, 2, 3, 1)
VMEM = pltpu.VMEM
F32 = jnp.float32
BF16 = jnp.bfloat16


def adam(values, moment_one, moment_two, gradient):
    moment_one = 0.9 * moment_one + 0.1 * gradient
    moment_two = 0.99 * moment_two + 0.01 * gradient * gradient
    values = values - learn_rate * moment_one / (jnp.sqrt(moment_two) + adam_eps)
    return values, moment_one, moment_two


def words(meta, stratum):
    return meta[stratum, 0, 0], meta[stratum, 1, 0]


def field(word, at, bits):
    return (word >> at) & ((1 << bits) - 1)


def row_of(rows, slot):
    return field(rows, 3 * slot, 3)


def col_of(rest, slot):
    return block_at(field(rest, 2 * slot, 2))


def live_of(rest):
    return field(rest, 16, 4)


def place_of(rest):
    return field(rest, 20, 2)


def block_at(index):
    return pl.ds(pl.multiple_of(index * EDGE, EDGE), EDGE)


def slot_grads(stratum, slots, meta, items, users, teacher, residual, grad):
    rows, rest = words(meta, stratum)
    blocks = [users[block_at(row_of(rows, slot)), :] for slot in range(slots)]
    for slot, user_block in enumerate(blocks):
        predicted = lax.dot_general(
            items[col_of(rest, slot), :], user_block, (((1,), (1,)), ((), ())), preferred_element_type=F32
        )
        scores = teacher[stratum, slot].T.astype(F32)
        residual[slot] = jnp.where(slot < live_of(rest), predicted - scores, 0.0).astype(BF16)
    stacked = jnp.concatenate(blocks, axis=0)
    for block in range(items.shape[0] // EDGE):
        hits = [
            jnp.where(field(rest, 2 * slot, 2) == block, residual[slot], jnp.zeros((), BF16)) for slot in range(slots)
        ]
        grad[block * EDGE : (block + 1) * EDGE, :] = jnp.dot(
            jnp.concatenate(hits, axis=1), stacked, preferred_element_type=F32
        )


def split_parts(place, grad, mine, *sent):
    shard = mine.shape[0] // 2
    for hop, part in zip((0, *SUM_HOPS), (mine, *sent)):
        start = pl.multiple_of((place ^ hop) * shard, shard)
        for side in range(2):
            rows = grad[pl.ds(start + side * OWNERS * shard, shard), :]
            part[side * shard : (side + 1) * shard, :] = rows.astype(part.dtype)


def first_item_kernel(stratum, slots, meta, items, users, teacher, *refs):
    *parts, residual, grad = refs
    slot_grads(stratum, slots, meta, items, users, teacher, residual, grad)
    split_parts(place_of(words(meta, stratum)[1]), grad, *parts)


def item_kernel(stratum, slots, meta, *refs):
    got = refs[:OWNERS]
    users, teacher, *parts, residual, items, grad = refs[OWNERS:]
    shard = items.shape[0] // (2 * OWNERS)
    place = place_of(words(meta, stratum)[1])
    for hop, piece in zip(HOPS, got):
        start = pl.multiple_of((place ^ hop) * shard, shard)
        for side in range(2):
            span = slice(side * shard, (side + 1) * shard)
            values = piece[span, :] if hop else piece[0, span, :].astype(BF16)
            items[pl.ds(start + side * OWNERS * shard, shard), :] = values
    slot_grads(stratum, slots, meta, items, users, teacher, residual, grad)
    split_parts(place, grad, *parts)


def user_grads(stratum, slots, meta, items, residual, grad):
    grad[...] = jnp.zeros_like(grad)
    rows, rest = words(meta, stratum)
    for slot in range(slots):
        col = col_of(rest, slot)
        grad[row_of(rows, slot)] += lax.dot_general(
            residual[slot], items[col, :], (((0,), (0,)), ((), ())), preferred_element_type=F32
        )


def user_kernel(stratum, slots, meta, items, residual, values, one, two, values_out, one_out, two_out, rounded, grad):
    user_grads(stratum, slots, meta, items, residual, grad)

    def one_block(at, carry):
        rows = block_at(at)
        new, first, second = adam(values[rows, :], one[rows, :], two[rows, :], grad[at])
        values_out[rows, :] = new
        one_out[rows, :] = first
        two_out[rows, :] = second
        rounded[rows, :] = new.astype(BF16)
        return carry

    lax.fori_loop(0, grad.shape[0], one_block, 0)


def last_user_kernel(stratum, slots, meta, items, residual, values, one, two, values_out, one_out, two_out, grad):
    at = pl.program_id(0)

    @pl.when(at == 0)
    def _():
        user_grads(stratum, slots, meta, items, residual, grad)

    values_out[...], one_out[...], two_out[...] = adam(
        values[...], one[...], two[...], grad[pl.ds(at * 2, 2)].reshape(values.shape)
    )


def sum_kernel(*refs):
    *parts, total = refs
    acc = parts[0][...]
    for part in parts[1:]:
        acc += part[...].astype(F32)
    total[...] = acc.astype(total.dtype)


def owner_kernel(mine, other, state, state_out, rounded):
    total = mine[...].astype(F32) + other[...].astype(F32)
    new, state_out[1], state_out[2] = adam(state[0], state[1], state[2], total)
    state_out[0] = new
    rounded[...] = new.astype(BF16)


def last_owner_kernel(stratum, slots, meta, mine, other, state, state_out):
    shard = state.shape[1] // 2
    rows = pl.ds(pl.multiple_of(field(words(meta, stratum)[1], 22, 1) * shard, shard), shard)
    total = mine[rows, :].astype(F32) + other[rows, :].astype(F32)
    state_out[0], state_out[1], state_out[2] = adam(state[0, rows, :], state[1, rows, :], state[2, rows, :], total)


def first_owner_kernel(slots, meta, mine, other_part, own, other, state_out, rounded):
    total = mine[...].astype(F32) + other_part[...].astype(F32)

    def update(low, high):
        columns = [jnp.concatenate([low[term], high[term]], axis=0) for term in range(3)]
        new, state_out[1], state_out[2] = adam(*columns, total)
        state_out[0] = new
        rounded[...] = new.astype(BF16)

    side = field(words(meta, 0)[1], 23, 1)

    @pl.when(side == 0)
    def _():
        update(own, other)

    @pl.when(side == 1)
    def _():
        update(other, own)


def start_kernel(values, one, two, own, arrived):
    moves = [
        pltpu.make_async_copy(source, own.at[term], arrived.at[term]) for term, source in enumerate((values, one, two))
    ]
    for move in moves:
        move.start()
    for move in moves:
        move.wait()


def finish_kernel(state, values, one, two, sent):
    moves = [
        pltpu.make_async_copy(state.at[term], target, sent.at[term]) for term, target in enumerate((values, one, two))
    ]
    for move in moves:
        move.start()
    for move in moves:
        move.wait()


def vmem_specs(count):
    return [pl.BlockSpec(memory_space=VMEM)] * count


def in_vmem(*arrays):
    return [pltpu.with_memory_space_constraint(a, VMEM) for a in arrays]


LIMIT = pltpu.CompilerParams(vmem_limit_bytes=6 * 1024 * 1024)
USER_COST = pl.CostEstimate(flops=300_000_000, bytes_accessed=8_000_000, transcendentals=600_000)


def on_device(
    user_factors,
    user_first,
    user_second,
    item_factors,
    item_first,
    item_second,
    block_rows,
    block_cols,
    live_slots,
    teacher,
):
    strata, slots = block_rows.shape[2], block_rows.shape[3]
    user_rows, rank = user_factors.shape
    shard = item_factors.shape[0]
    groups, reps = lax.axis_size("blk"), lax.axis_size("rep")
    item_rows = shard * reps

    def moves(hop):
        return [
            (group * reps + rep, ((group - 1) % groups) * reps + (rep ^ hop ^ (0 if group % 2 else OWNERS)))
            for group in range(groups)
            for rep in range(reps)
        ]

    def shifted(value, hop=0):
        return lax.ppermute(value, ("blk", "rep"), moves(hop))

    rep = lax.axis_index("rep")
    side = rep // OWNERS
    keep = (side + 1 - lax.axis_index("blk") % 2) % 2
    slot_at = jnp.arange(slots, dtype=jnp.int32)
    row_words = jnp.sum(block_rows[0, 0] << (3 * slot_at), axis=1)
    col_words = jnp.sum(block_cols[0, 0] << (2 * slot_at), axis=1)
    col_words += (live_slots[0, 0] << 16) + ((rep % OWNERS) << 20) + (keep << 22) + (side << 23)
    meta = jnp.broadcast_to(jnp.stack([row_words, col_words], axis=1)[:, :, None], (strata, 2, EDGE))

    scores = teacher[0, 0]
    users = (user_factors, user_first, user_second)

    anywhere = pl.BlockSpec(memory_space=pl.ANY)
    own = pl.pallas_call(
        start_kernel,
        in_specs=[anywhere] * 3,
        out_specs=vmem_specs(1)[0],
        out_shape=VMEM((3, shard, rank), F32),
        scratch_shapes=[pltpu.SemaphoreType.DMA((3,))],
        compiler_params=LIMIT,
        name="start",
    )(*[pltpu.with_memory_space_constraint(a, pltpu.HBM) for a in (item_factors, item_first, item_second)])
    other = lax.ppermute(own, "rep", [(at, at ^ OWNERS) for at in range(reps)])
    copies = jnp.broadcast_to(own[0].astype(BF16)[None], (reps, shard, rank))
    items = lax.all_to_all(copies, "rep", 0, 0).reshape(item_rows, rank)
    items, own, other, meta, factors = lax.optimization_barrier((items, own, other, meta, user_factors))
    user_bf = factors.astype(BF16)

    parts_shape = [VMEM((2 * shard, rank), F32)] + [VMEM((2 * shard, rank), BF16)] * (OWNERS - 1)
    item_scratch = [VMEM((item_rows, rank), F32)]
    residual_shape = VMEM((slots, EDGE, EDGE), BF16)
    for stratum in range(strata):
        last = stratum == strata - 1
        if stratum == 0:
            *parts, residual = pl.pallas_call(
                functools.partial(first_item_kernel, stratum, slots),
                in_specs=vmem_specs(1 + 3),
                out_specs=vmem_specs(OWNERS + 1),
                out_shape=[*parts_shape, residual_shape],
                scratch_shapes=item_scratch,
                compiler_params=LIMIT,
                name="item_grad",
            )(*in_vmem(meta, items, user_bf, scores))
        else:
            *parts, residual, items = pl.pallas_call(
                functools.partial(item_kernel, stratum, slots),
                in_specs=vmem_specs(1 + OWNERS + 2),
                out_specs=vmem_specs(OWNERS + 2),
                out_shape=[*parts_shape, residual_shape, VMEM((item_rows, rank), BF16)],
                scratch_shapes=item_scratch,
                compiler_params=LIMIT,
                name="item_grad",
            )(*in_vmem(meta, *got, user_bf, scores))
        for at, hop in enumerate(SUM_HOPS):
            parts[at + 1] = lax.ppermute(parts[at + 1], "rep", [(rep, rep ^ hop) for rep in range(reps)])
        mine = pl.pallas_call(
            sum_kernel,
            in_specs=vmem_specs(OWNERS),
            out_specs=vmem_specs(1)[0],
            out_shape=VMEM((2 * shard, rank), BF16),
            compiler_params=LIMIT,
            name="sum_parts",
        )(*in_vmem(*parts))
        partner = lax.ppermute(mine, "rep", [(at, at ^ OWNERS) for at in range(reps)])
        scratch = [VMEM((user_rows // EDGE, EDGE, rank), F32)]
        if last:
            state = pl.pallas_call(
                functools.partial(last_owner_kernel, stratum, slots),
                in_specs=vmem_specs(1 + 3),
                out_specs=vmem_specs(1)[0],
                out_shape=VMEM((3, shard, rank), F32),
                compiler_params=LIMIT,
                name="owner_adam",
            )(*in_vmem(meta, mine, partner, state))
            residual, state = lax.optimization_barrier((residual, state))
            state = shifted(state)
            by_block = pl.BlockSpec((2 * EDGE, rank), lambda at: (at, 0))
            users = pl.pallas_call(
                functools.partial(last_user_kernel, stratum, slots),
                grid=(user_rows // (2 * EDGE),),
                in_specs=vmem_specs(1 + 2) + [by_block] * 3,
                out_specs=[by_block] * 3,
                out_shape=[jax.ShapeDtypeStruct((user_rows, rank), F32)] * 3,
                scratch_shapes=scratch,
                compiler_params=LIMIT,
                cost_estimate=USER_COST,
                name="last_user_adam",
            )(*in_vmem(meta, items, residual), *users)
        else:
            first = stratum == 0
            state, rounded = pl.pallas_call(
                functools.partial(first_owner_kernel, slots) if first else owner_kernel,
                in_specs=vmem_specs(5 if first else 3),
                out_specs=vmem_specs(2),
                out_shape=[VMEM((3, 2 * shard, rank), F32), VMEM((2 * shard, rank), BF16)],
                compiler_params=LIMIT,
                name="owner_adam",
            )(*in_vmem(*[meta] * first, mine, partner, *((own, other) if first else (state,))))
            residual, rounded, state = lax.optimization_barrier((residual, rounded, state))
            got = [shifted(rounded, hop) if hop else None for hop in HOPS]
            state = shifted(state)
            got[HOPS.index(0)] = state
            *users, user_bf = pl.pallas_call(
                functools.partial(user_kernel, stratum, slots),
                in_specs=vmem_specs(1 + 5),
                out_specs=vmem_specs(4),
                out_shape=[VMEM((user_rows, rank), kind) for kind in (F32, F32, F32, BF16)],
                scratch_shapes=scratch,
                compiler_params=LIMIT,
                cost_estimate=USER_COST,
                name="user_adam",
            )(*in_vmem(meta, items, residual, *users))

    items = pl.pallas_call(
        finish_kernel,
        in_specs=vmem_specs(1),
        out_specs=[anywhere] * 3,
        out_shape=[pltpu.HBM((shard, rank), F32)] * 3,
        scratch_shapes=[pltpu.SemaphoreType.DMA((3,))],
        compiler_params=LIMIT,
        name="finish",
    )(*in_vmem(state))
    return (*users, *items)


def solution(mesh):
    rows = P(("blk", "rep"), None)
    in_specs = (rows,) * 6 + (
        P("blk", "rep", None, None),
        P("blk", "rep", None, None),
        P("blk", "rep", None),
        P("blk", "rep", None, None, None, None),
    )
    return jax.shard_map(on_device, mesh=mesh, in_specs=in_specs, out_specs=(rows,) * 6, check_vma=False)
```
